128 devices in a mesh: row: 8 (over z, core), col: 16 (over x, y).
Axes of the slice: x: 4, y: 4, z: 4, core: 2. Of those that a mesh axis runs over, the one named last changes fastest.
Arguments:
- amplitudes: float32 [16, 160, 256, 256], P('row', None, 'col'), may hold values from -6 to 6
- integrals: float32 [160, 256, 2560], P('row', 'col'), may hold values from -0.03125 to 0.03125
- occ_irrep: int32 [150], replicated, may hold values from 0 to 7, as said below
- vir_irrep: int32 [1500], replicated, may hold values from 0 to 7, as said below
Outputs:
- cycle_term: float32 [16, 256, 2560], P('row', 'col')
The draws below stay inside these ranges and needn't reach their ends.
Inputs may be any that keep to these rules, and one draw needn't show every extreme that they name: `occ_irrep`: nondecreasing. `vir_irrep`: nondecreasing; no label is carried by more than 256 virtual orbitals, and some label is carried by exactly 256.
All inputs are finite; a program needn't handle non-finite values.
Results may differ from the reference program's by a relative error of at most 0.00007.
Values sent between devices are 32-bit elements; how exact they have to be, the bound alone decides.
No kernel may reach another device: no remote copies, remote signals or barrier semaphores. Data moves between devices by JAX's collectives and lax.ppermute only.
A program may use at most 192 MiB of HBM per device.

```python
import jax
import jax.numpy as jnp
from jax import lax

O = 150
V = 1500
VCAP = 256
OSLOT = 160
OW = 16
NCOL = 2560


def draw_occ_irrep(key, part):
    key = jax.random.fold_in(key, 3)
    labels = jax.random.randint(key, (O,), 0, 8, dtype=jnp.int32)
    return jnp.sort(labels)


def draw_vir_irrep(key, part):
    key = jax.random.fold_in(key, 7)
    subkeys = jax.random.split(key, 4)
    remainder = V - VCAP
    base_count = remainder // 7
    leftover = remainder % 7
    spread = max(0, min(base_count, VCAP - base_count - 1))
    largest = jax.random.randint(subkeys[0], (), 0, 8, dtype=jnp.int32)
    swings = jax.random.randint(subkeys[1], (3,), 0, spread + 1, dtype=jnp.int32)
    changes = jnp.concatenate([swings, -swings, jnp.zeros((1,), jnp.int32)])
    changes = changes[jax.random.permutation(subkeys[2], 7)]
    extras = (jnp.arange(7, dtype=jnp.int32) < leftover).astype(jnp.int32)
    extras = extras[jax.random.permutation(subkeys[3], 7)]
    others = base_count + changes + extras
    position = jnp.arange(8, dtype=jnp.int32)
    other_slot = jnp.clip(position - (position > largest).astype(jnp.int32), 0, 6)
    block_counts = jnp.where(position == largest, VCAP, others[other_slot])
    block_ends = jnp.cumsum(block_counts)
    orbital = jnp.arange(V, dtype=jnp.int32)
    return jnp.sum((orbital[:, None] >= block_ends[None, :]).astype(jnp.int32), axis=1).astype(jnp.int32)


def shard_levels(rng, extent, cuts, smallest, high):
    loudness = 1.0
    for dim, shards_of in cuts:
        draws = jax.random.uniform(jax.random.fold_in(jax.random.fold_in(rng, 6), dim), (shards_of,), jnp.float32, smallest / len(cuts), high / len(cuts))
        loudness = loudness * jnp.repeat(jnp.exp(draws), extent[dim] // shards_of).reshape((-1,) + (1,) * (len(extent) - 1 - dim))
    return loudness


def centred(stream_key, shape, scale, most, cuts=(), kind=jnp.bfloat16):
    result = jax.random.normal(stream_key, shape, jnp.float32) * scale
    if len(cuts) > 0:
        result = shard_levels(stream_key, shape, cuts, -0.22, 0.18) * result
    return jnp.clip(result, min=-most, max=most).astype(kind)


def setup_inputs(seed: int = 0) -> dict:
    streams_of = jax.random.split(jax.random.key(seed), 5)
    amplitudes = centred(streams_of[0], (OW, OSLOT, VCAP, VCAP), 1.0, 6.0, ((0, 8), (2, 16)), jnp.float32)
    integrals = centred(streams_of[1], (OSLOT, VCAP, NCOL), (O * V // 8) ** -0.5, 0.03125, ((0, 8), (1, 16)), jnp.float32)
    occ_irrep = draw_occ_irrep(jax.random.fold_in(streams_of[4], 71), 0)
    vir_irrep = draw_vir_irrep(jax.random.fold_in(streams_of[4], 71), 0)
    return {"amplitudes": amplitudes, "integrals": integrals, "occ_irrep": occ_irrep, "vir_irrep": vir_irrep}


def irrep_counts(vir_irrep):
    labels = jnp.arange(8, dtype=jnp.int32)
    return jnp.sum((vir_irrep[:, None] == labels[None, :]).astype(jnp.int32), axis=0)


def block_sizes(orbital_irreps, counts):
    labels = jnp.arange(8, dtype=jnp.int32)
    return jnp.sum(jnp.where(orbital_irreps[:, None] == labels[None, :], counts[None, :], 0), axis=1)


def reference(amplitudes, integrals, occ_irrep, vir_irrep):
    counts = irrep_counts(vir_irrep)
    padded = jnp.concatenate([occ_irrep, jnp.zeros((OSLOT - O,), jnp.int32)])
    slot_index = jnp.arange(OSLOT, dtype=jnp.int32)
    column_sizes = jnp.where(slot_index < O, block_sizes(padded, counts), 0)
    virtual = jnp.arange(VCAP, dtype=jnp.int32)
    colmask = (virtual[None, :] < column_sizes[:, None]).astype(jnp.float32)
    window = (jnp.arange(OW, dtype=jnp.int32) * O) // OW
    row_sizes = block_sizes(occ_irrep[window], counts)
    rowmask = (virtual[None, :] < row_sizes[:, None]).astype(jnp.float32)
    masked = integrals * colmask[:, :, None]

    def one_orbital(amplitude_block):
        return jnp.einsum("kac,kcn->an", amplitude_block, masked, precision=lax.Precision.HIGHEST)

    cycle_term = lax.map(one_orbital, amplitudes)
    return cycle_term * rowmask[:, :, None]
```

```python
import functools

import jax
import jax.numpy as jnp
from jax import lax
from jax.experimental import pallas as pl
from jax.experimental.pallas import tpu as pltpu
from jax.sharding import PartitionSpec as P

WIDTHS = (1024, 1024, 512)
TILE = 256
LANES = 128
MIB = 1024 * 1024


def irrep_counts(vir_irrep):
    labels = jnp.arange(8, dtype=jnp.int32)
    return jnp.sum((vir_irrep[:, None] == labels[None, :]).astype(jnp.int32), axis=0)


def block_sizes(orbital_irreps, counts):
    labels = jnp.arange(8, dtype=jnp.int32)
    return jnp.sum(
        jnp.where(orbital_irreps[:, None] == labels[None, :], counts[None, :], 0), axis=1
    )


def masks(slot_total, local_orbitals, local_columns, occ_irrep, vir_irrep):
    occupied = occ_irrep.shape[0]
    window_total = local_orbitals * lax.axis_size("row")
    counts = irrep_counts(vir_irrep)
    sizes = jnp.pad(block_sizes(occ_irrep, counts), (0, slot_total - occupied))
    local = lax.axis_index("col") * local_columns + jnp.arange(local_columns, dtype=jnp.int32)
    colmask = (local[None, :] < sizes[:, None]).astype(jnp.float32).reshape(1, slot_total * local_columns)
    window = lax.axis_index("row") * local_orbitals + jnp.arange(local_orbitals, dtype=jnp.int32)
    orbital = window * occupied // window_total
    matches = jnp.arange(occupied, dtype=jnp.int32)[None, :] == orbital[:, None]
    row_sizes = block_sizes(jnp.sum(jnp.where(matches, occ_irrep[None, :], 0), axis=1), counts)
    return colmask, row_sizes


def pack_kernel(order_ref, first_ref, second_ref, out_ref, *, width):
    slots, rows, columns = first_ref.shape[1:]
    per = LANES // width
    place = lax.broadcasted_iota(jnp.int32, (rows, LANES), 1) // width
    for group in range(2 * slots // per):
        for half in range(columns // LANES):
            at = slice(half * LANES, (half + 1) * LANES)
            tiles = []
            for k in range(per):
                slot = group * per + k
                ref = first_ref if slot < slots else second_ref
                tile = ref[0, slot % slots, :, at]
                tiles.append(pltpu.roll(tile, k * width, 1) if k else tile)
            span = 1
            while span < per:
                taken = place & span != 0
                tiles = [jnp.where(taken, tiles[(h + span) % per], tiles[h]) for h in range(per)]
                span *= 2
            for g in range(per):
                tile = tiles[-g % per]
                tile = pltpu.roll(tile, LANES - g * width, 1) if g else tile
                out_ref[half * per + g, :, group * LANES:(group + 1) * LANES] = tile


def pack(amplitudes, order, slots, width, orbital):
    wl, kt, al, ct = amplitudes.shape
    return pl.pallas_call(
        functools.partial(pack_kernel, width=width),
        grid_spec=pltpu.PrefetchScalarGridSpec(
            num_scalar_prefetch=1,
            grid=(kt // slots // 2,),
            in_specs=[
                pl.BlockSpec((1, slots, al, ct), lambda p, o: (orbital, o[2 * p], 0, 0)),
                pl.BlockSpec((1, slots, al, ct), lambda p, o: (orbital, o[2 * p + 1], 0, 0)),
            ],
            out_specs=pl.BlockSpec((ct // width, al, 2 * slots * width), lambda p, o: (0, 0, p)),
        ),
        out_shape=jax.ShapeDtypeStruct((ct // width, al, kt * width), jnp.float32),
        compiler_params=pltpu.CompilerParams(vmem_limit_bytes=56 * MIB),
        cost_estimate=pl.CostEstimate(
            flops=kt * al * ct, bytes_accessed=8 * kt * al * ct, transcendentals=0
        ),
    )(order, amplitudes, amplitudes)


def split(value):
    high = value.astype(jnp.bfloat16)
    return high, (value - high.astype(jnp.float32)).astype(jnp.bfloat16)


def prepare_kernel(size_ref, left_ref, mask_ref, high_ref, low_ref):
    block = left_ref.shape[0]
    row = pl.program_id(0) * block + lax.broadcasted_iota(jnp.int32, (block, 1), 0)
    keep = (row < size_ref[0]).astype(jnp.float32)
    high_ref[...], low_ref[...] = split(left_ref[...] * mask_ref[...] * keep)


def prepare(left, colmask, size):
    col, al, depth = left.shape
    rows, block = col * al, 64
    return pl.pallas_call(
        prepare_kernel,
        grid_spec=pltpu.PrefetchScalarGridSpec(
            num_scalar_prefetch=1,
            grid=(rows // block,),
            in_specs=[
                pl.BlockSpec((block, depth), lambda n, *_: (n, 0)),
                pl.BlockSpec((1, depth), lambda n, *_: (0, 0)),
            ],
            out_specs=[pl.BlockSpec((block, depth), lambda n, *_: (n, 0))] * 2,
        ),
        out_shape=[jax.ShapeDtypeStruct((rows, depth), jnp.bfloat16)] * 2,
        compiler_params=pltpu.CompilerParams(vmem_limit_bytes=56 * MIB),
        cost_estimate=pl.CostEstimate(flops=4 * rows * depth, bytes_accessed=8 * rows * depth, transcendentals=0),
    )(size, left.reshape(rows, depth), colmask)


def multiply_kernel(*refs, panels, lefts):
    order_ref, left_refs = refs[0], refs[1:1 + 2 * lefts]
    panel_refs, out_ref = refs[1 + 2 * lefts:-1], refs[-1]
    del order_ref
    high, low = split(jnp.concatenate([ref[...].reshape(ref.shape[-2:]) for ref in panel_refs], axis=0))
    dot = functools.partial(jnp.dot, preferred_element_type=jnp.float32)
    for i in range(lefts):
        left_high, left_low = left_refs[2 * i], left_refs[2 * i + 1]
        total = dot(left_high[...], high) + (dot(left_high[...], low) + dot(left_low[...], high))
        out_ref[:, i] = total.reshape(out_ref.shape[0], *out_ref.shape[2:])


def multiply(order, lefts, panels, virtuals):
    rows, depth = lefts[0].shape
    width = panels[0].shape[-1]
    count = len(lefts) // 2
    if len(panels) == 1:
        blocks = panels[0].shape[0]
        panels = panels * blocks
        specs = [
            pl.BlockSpec((1, depth // blocks, TILE), lambda n, o, i=i: (o[i], 0, n)) for i in range(blocks)
        ]
    else:
        specs = [pl.BlockSpec((panel.shape[0], TILE), lambda n, o: (0, n)) for panel in panels]
    shape = (rows // virtuals, count, virtuals)
    return pl.pallas_call(
        functools.partial(multiply_kernel, panels=len(panels), lefts=count),
        grid_spec=pltpu.PrefetchScalarGridSpec(
            num_scalar_prefetch=1,
            grid=(width // TILE,),
            in_specs=[pl.BlockSpec((rows, depth), lambda n, o: (0, 0))] * (2 * count) + specs,
            out_specs=pl.BlockSpec((*shape, TILE), lambda n, o: (0, 0, 0, n)),
        ),
        out_shape=jax.ShapeDtypeStruct((*shape, width), jnp.float32),
        compiler_params=pltpu.CompilerParams(vmem_limit_bytes=56 * MIB),
        cost_estimate=pl.CostEstimate(
            flops=6 * count * rows * depth * width,
            bytes_accessed=4 * (count * rows * depth + depth * width + count * rows * width),
            transcendentals=0,
        ),
    )(order, *lefts, *panels)


def body(amplitudes, integrals, occ_irrep, vir_irrep):
    rows, col = lax.axis_size("row"), lax.axis_size("col")
    wl, kt, al, ct = amplitudes.shape
    kl, cl, nt = integrals.shape
    chips = rows // 2
    here = lax.axis_index("row")
    chip, core = here // 2, here % 2
    order = jnp.stack(
        [(chip + s) % chips * 2 + c for c in (core, 1 - core) for s in (0, chips - 1, 1, 2)]
    ).astype(jnp.int32)
    colmask, row_sizes = masks(kt, wl, cl, occ_irrep, vir_irrep)
    colmask = colmask.reshape(rows, kl * cl)
    colmask = jnp.concatenate([lax.dynamic_slice_in_dim(colmask, order[i], 1) for i in range(rows)], axis=1)
    starts = [sum(WIDTHS[:i]) for i in range(len(WIDTHS))]
    own = [integrals[:, :, s:s + n] for s, n in zip(starts, WIDTHS)]

    def to_rows(value):
        return lax.all_to_all(value, "col", split_axis=0, concat_axis=0, tiled=True)

    panels = [lax.all_gather(value, "row", axis=0, tiled=True).reshape(rows, kl * cl, -1) for value in own]
    halves = []
    for w in range(wl):
        left = to_rows(pack(amplitudes, order, kl, cl, w))
        halves += prepare(left, colmask, row_sizes[w:w + 1])
    pieces = []
    for panel in panels:
        pieces.append(jnp.sum(to_rows(multiply(order, halves, [panel], al)), axis=0))
    return jnp.concatenate(pieces, axis=2)


def solution(mesh):
    return jax.shard_map(
        body,
        mesh=mesh,
        in_specs=(P("row", None, "col", None), P("row", "col", None), P(), P()),
        out_specs=P("row", "col", None),
        check_vma=False,
    )
```

```python
import functools

import jax
import jax.numpy as jnp
from jax import lax
from jax.experimental import pallas as pl
from jax.experimental.pallas import tpu as pltpu
from jax.sharding import PartitionSpec as P

WIDTHS = (1536, 1024)
TILE = 256
LANES = 128
MIB = 1024 * 1024


def irrep_counts(vir_irrep):
    labels = jnp.arange(8, dtype=jnp.int32)
    return jnp.sum((vir_irrep[:, None] == labels[None, :]).astype(jnp.int32), axis=0)


def block_sizes(orbital_irreps, counts):
    labels = jnp.arange(8, dtype=jnp.int32)
    return jnp.sum(
        jnp.where(orbital_irreps[:, None] == labels[None, :], counts[None, :], 0), axis=1
    )


def masks(slot_total, local_orbitals, local_columns, occ_irrep, vir_irrep):
    occupied = occ_irrep.shape[0]
    window_total = local_orbitals * lax.axis_size("row")
    counts = irrep_counts(vir_irrep)
    sizes = jnp.pad(block_sizes(occ_irrep, counts), (0, slot_total - occupied))
    local = lax.axis_index("col") * local_columns + jnp.arange(local_columns, dtype=jnp.int32)
    colmask = (local[None, :] < sizes[:, None]).astype(jnp.float32).reshape(1, slot_total * local_columns)
    window = lax.axis_index("row") * local_orbitals + jnp.arange(local_orbitals, dtype=jnp.int32)
    orbital = window * occupied // window_total
    matches = jnp.arange(occupied, dtype=jnp.int32)[None, :] == orbital[:, None]
    row_sizes = block_sizes(jnp.sum(jnp.where(matches, occ_irrep[None, :], 0), axis=1), counts)
    return colmask, row_sizes


def pack_kernel(order_ref, first_ref, second_ref, out_ref, *, width):
    slots, rows, columns = first_ref.shape[1:]
    per = LANES // width
    place = lax.broadcasted_iota(jnp.int32, (rows, LANES), 1) // width
    for group in range(2 * slots // per):
        for half in range(columns // LANES):
            at = slice(half * LANES, (half + 1) * LANES)
            tiles = []
            for k in range(per):
                slot = group * per + k
                ref = first_ref if slot < slots else second_ref
                tile = ref[0, slot % slots, :, at]
                tiles.append(pltpu.roll(tile, k * width, 1) if k else tile)
            span = 1
            while span < per:
                taken = place & span != 0
                tiles = [jnp.where(taken, tiles[(h + span) % per], tiles[h]) for h in range(per)]
                span *= 2
            for g in range(per):
                tile = tiles[-g % per]
                tile = pltpu.roll(tile, LANES - g * width, 1) if g else tile
                out_ref[half * per + g, :, group * LANES:(group + 1) * LANES] = tile


def pack(amplitudes, order, slots, width, orbital):
    wl, kt, al, ct = amplitudes.shape
    return pl.pallas_call(
        functools.partial(pack_kernel, width=width),
        grid_spec=pltpu.PrefetchScalarGridSpec(
            num_scalar_prefetch=1,
            grid=(kt // slots // 2,),
            in_specs=[
                pl.BlockSpec((1, slots, al, ct), lambda p, o: (orbital, o[2 * p], 0, 0)),
                pl.BlockSpec((1, slots, al, ct), lambda p, o: (orbital, o[2 * p + 1], 0, 0)),
            ],
            out_specs=pl.BlockSpec((ct // width, al, 2 * slots * width), lambda p, o: (0, 0, p)),
        ),
        out_shape=jax.ShapeDtypeStruct((ct // width, al, kt * width), jnp.float32),
        compiler_params=pltpu.CompilerParams(vmem_limit_bytes=56 * MIB),
        cost_estimate=pl.CostEstimate(
            flops=kt * al * ct, bytes_accessed=8 * kt * al * ct, transcendentals=0
        ),
    )(order, amplitudes, amplitudes)


def split(value):
    high = value.astype(jnp.bfloat16)
    return high, (value - high.astype(jnp.float32)).astype(jnp.bfloat16)


def prepare_kernel(size_ref, left_ref, mask_ref, high_ref, low_ref):
    block = left_ref.shape[0]
    row = pl.program_id(0) * block + lax.broadcasted_iota(jnp.int32, (block, 1), 0)
    keep = (row < size_ref[0]).astype(jnp.float32)
    high_ref[...], low_ref[...] = split(left_ref[...] * mask_ref[...] * keep)


def prepare(left, colmask, size):
    col, al, depth = left.shape
    rows, block = col * al, 128
    return pl.pallas_call(
        prepare_kernel,
        grid_spec=pltpu.PrefetchScalarGridSpec(
            num_scalar_prefetch=1,
            grid=(rows // block,),
            in_specs=[
                pl.BlockSpec((block, depth), lambda n, *_: (n, 0)),
                pl.BlockSpec((1, depth), lambda n, *_: (0, 0)),
            ],
            out_specs=[pl.BlockSpec((block, depth), lambda n, *_: (n, 0))] * 2,
        ),
        out_shape=[jax.ShapeDtypeStruct((rows, depth), jnp.bfloat16)] * 2,
        compiler_params=pltpu.CompilerParams(vmem_limit_bytes=56 * MIB),
        cost_estimate=pl.CostEstimate(flops=4 * rows * depth, bytes_accessed=8 * rows * depth, transcendentals=0),
    )(size, left.reshape(rows, depth), colmask)


def multiply_kernel(*refs, panels, lefts):
    order_ref, left_refs = refs[0], refs[1:1 + 2 * lefts]
    panel_refs, out_ref = refs[1 + 2 * lefts:-1], refs[-1]
    del order_ref
    high, low = split(jnp.concatenate([ref[...].reshape(ref.shape[-2:]) for ref in panel_refs], axis=0))
    dot = functools.partial(jnp.dot, preferred_element_type=jnp.float32)
    for i in range(lefts):
        left_high, left_low = left_refs[2 * i], left_refs[2 * i + 1]
        total = dot(left_high[...], high) + (dot(left_high[...], low) + dot(left_low[...], high))
        out_ref[:, i] = total.reshape(out_ref.shape[0], *out_ref.shape[2:])


def multiply(order, lefts, panels, virtuals):
    rows, depth = lefts[0].shape
    width = panels[0].shape[-1]
    count = len(lefts) // 2
    if len(panels) == 1:
        blocks = panels[0].shape[0]
        panels = panels * blocks
        specs = [
            pl.BlockSpec((1, depth // blocks, TILE), lambda n, o, i=i: (o[i], 0, n)) for i in range(blocks)
        ]
    else:
        specs = [pl.BlockSpec((panel.shape[0], TILE), lambda n, o: (0, n)) for panel in panels]
    shape = (rows // virtuals, count, virtuals)
    return pl.pallas_call(
        functools.partial(multiply_kernel, panels=len(panels), lefts=count),
        grid_spec=pltpu.PrefetchScalarGridSpec(
            num_scalar_prefetch=1,
            grid=(width // TILE,),
            in_specs=[pl.BlockSpec((rows, depth), lambda n, o: (0, 0))] * (2 * count) + specs,
            out_specs=pl.BlockSpec((*shape, TILE), lambda n, o: (0, 0, 0, n)),
        ),
        out_shape=jax.ShapeDtypeStruct((*shape, width), jnp.float32),
        compiler_params=pltpu.CompilerParams(vmem_limit_bytes=56 * MIB),
        cost_estimate=pl.CostEstimate(
            flops=6 * count * rows * depth * width,
            bytes_accessed=4 * (count * rows * depth + depth * width + count * rows * width),
            transcendentals=0,
        ),
    )(order, *lefts, *panels)


def body(amplitudes, integrals, occ_irrep, vir_irrep):
    rows, col = lax.axis_size("row"), lax.axis_size("col")
    wl, kt, al, ct = amplitudes.shape
    kl, cl, nt = integrals.shape
    part, chips = kl // 2, rows // 2
    cross = [(r, r ^ 1) for r in range(rows)]
    up = [(r, (r + 2) % rows) for r in range(rows)]
    down = [(r, (r - 2) % rows) for r in range(rows)]
    here = lax.axis_index("row")
    chip, core = here // 2, here % 2
    order = jnp.stack(
        [(chip + s) % chips * 2 + c for c in (core, 1 - core) for s in (0, chips - 1, 1, 2)]
    ).astype(jnp.int32)

    def to_rows(value):
        return lax.all_to_all(value, "col", split_axis=0, concat_axis=0, tiled=True)

    def ring(value):
        return [lax.ppermute(value, "row", up), lax.ppermute(value, "row", down)]

    def ring_on(near):
        return [lax.ppermute(near[0][:part], "row", up), lax.ppermute(near[1][part:], "row", down)]

    def other_core(values):
        return [lax.ppermute(value, "row", cross) for value in values]

    def flat(*panels):
        return [panel.reshape(-1, panel.shape[-1]) for panel in panels]

    packed = [pack(amplitudes, order, kl, cl, w) for w in range(wl)]
    late, early = integrals[:, :, :WIDTHS[1]], integrals[:, :, WIDTHS[1]:]
    near0 = ring(early)
    near0, packed[1] = lax.optimization_barrier((near0, packed[1]))
    far0 = ring_on(near0)
    over0 = other_core([early, *near0])
    (late, far0, over0) = lax.optimization_barrier((late, far0, over0))
    near1 = ring(late)
    over0 += other_core(far0)
    colmask, row_sizes = masks(kt, wl, cl, occ_irrep, vir_irrep)
    colmask = colmask.reshape(rows, kl * cl)
    colmask = jnp.concatenate([lax.dynamic_slice_in_dim(colmask, order[i], 1) for i in range(rows)], axis=1)
    left0 = to_rows(packed[0])
    packed[1], left0 = lax.optimization_barrier((packed[1], left0))
    left1 = to_rows(packed[1])
    halves = prepare(left0, colmask, row_sizes[0:1])
    panels = flat(early, *near0, *far0, *over0)
    piece0 = multiply(order, halves, panels, al)
    moved0 = to_rows(lax.optimization_barrier((piece0, left1))[0])
    halves = halves + prepare(left1, colmask, row_sizes[1:2])
    piece1 = multiply(order, halves[2:], panels, al)
    near1 = lax.optimization_barrier((near1, piece0, halves[2:]))[0]
    far1 = ring_on(near1)
    over1 = other_core([late, *near1])
    far1 = lax.optimization_barrier((far1, piece1))[0]
    over1 += other_core(far1)
    moved1 = to_rows(lax.optimization_barrier((piece1, moved0))[0])
    last = multiply(order, halves, flat(late, *near1, *far1, *over1), al)
    last = lax.optimization_barrier((last, moved1))[0]
    sums = [jnp.sum(moved, axis=0) for moved in (moved0, moved1)]
    last = jnp.sum(to_rows(last), axis=0)
    return jnp.concatenate([last, jnp.concatenate(sums, axis=0)], axis=2)


def solution(mesh):
    return jax.shard_map(
        body,
        mesh=mesh,
        in_specs=(P("row", None, "col", None), P("row", "col", None), P(), P()),
        out_specs=P("row", "col", None),
        check_vma=False,
    )
```

```python
import functools

import jax
import jax.numpy as jnp
from jax import lax
from jax.experimental import pallas as pl
from jax.experimental.pallas import tpu as pltpu
from jax.sharding import PartitionSpec as P

WIDTHS = (1536, 1024)
TILE = 256
LANES = 128
MIB = 1024 * 1024


def irrep_counts(vir_irrep):
    labels = jnp.arange(8, dtype=jnp.int32)
    return jnp.sum((vir_irrep[:, None] == labels[None, :]).astype(jnp.int32), axis=0)


def block_sizes(orbital_irreps, counts):
    labels = jnp.arange(8, dtype=jnp.int32)
    return jnp.sum(
        jnp.where(orbital_irreps[:, None] == labels[None, :], counts[None, :], 0), axis=1
    )


def masks(slot_total, local_orbitals, local_columns, occ_irrep, vir_irrep):
    occupied = occ_irrep.shape[0]
    window_total = local_orbitals * lax.axis_size("row")
    counts = irrep_counts(vir_irrep)
    sizes = jnp.pad(block_sizes(occ_irrep, counts), (0, slot_total - occupied))
    local = lax.axis_index("col") * local_columns + jnp.arange(local_columns, dtype=jnp.int32)
    colmask = (local[None, :] < sizes[:, None]).astype(jnp.float32).reshape(1, slot_total * local_columns)
    window = lax.axis_index("row") * local_orbitals + jnp.arange(local_orbitals, dtype=jnp.int32)
    orbital = window * occupied // window_total
    matches = jnp.arange(occupied, dtype=jnp.int32)[None, :] == orbital[:, None]
    row_sizes = block_sizes(jnp.sum(jnp.where(matches, occ_irrep[None, :], 0), axis=1), counts)
    return colmask, row_sizes


def pack_kernel(order_ref, first_ref, second_ref, out_ref, *, width):
    slots, rows, columns = first_ref.shape[1:]
    per = LANES // width
    place = lax.broadcasted_iota(jnp.int32, (rows, LANES), 1) // width
    for group in range(2 * slots // per):
        for half in range(columns // LANES):
            at = slice(half * LANES, (half + 1) * LANES)
            tiles = []
            for k in range(per):
                slot = group * per + k
                ref = first_ref if slot < slots else second_ref
                tile = ref[0, slot % slots, :, at]
                tiles.append(pltpu.roll(tile, k * width, 1) if k else tile)
            span = 1
            while span < per:
                taken = place & span != 0
                tiles = [jnp.where(taken, tiles[(h + span) % per], tiles[h]) for h in range(per)]
                span *= 2
            for g in range(per):
                tile = tiles[-g % per]
                tile = pltpu.roll(tile, LANES - g * width, 1) if g else tile
                out_ref[half * per + g, :, group * LANES:(group + 1) * LANES] = tile


def pack(amplitudes, order, slots, width, orbital):
    wl, kt, al, ct = amplitudes.shape
    return pl.pallas_call(
        functools.partial(pack_kernel, width=width),
        grid_spec=pltpu.PrefetchScalarGridSpec(
            num_scalar_prefetch=1,
            grid=(kt // slots // 2,),
            in_specs=[
                pl.BlockSpec((1, slots, al, ct), lambda p, o: (orbital, o[2 * p], 0, 0)),
                pl.BlockSpec((1, slots, al, ct), lambda p, o: (orbital, o[2 * p + 1], 0, 0)),
            ],
            out_specs=pl.BlockSpec((ct // width, al, 2 * slots * width), lambda p, o: (0, 0, p)),
        ),
        out_shape=jax.ShapeDtypeStruct((ct // width, al, kt * width), jnp.float32),
        compiler_params=pltpu.CompilerParams(vmem_limit_bytes=56 * MIB),
        cost_estimate=pl.CostEstimate(
            flops=kt * al * ct, bytes_accessed=8 * kt * al * ct, transcendentals=0
        ),
    )(order, amplitudes, amplitudes)


def split(value):
    high = value.astype(jnp.bfloat16)
    return high, (value - high.astype(jnp.float32)).astype(jnp.bfloat16)


def prepare_kernel(size_ref, left_ref, mask_ref, high_ref, low_ref):
    block = left_ref.shape[0]
    row = pl.program_id(0) * block + lax.broadcasted_iota(jnp.int32, (block, 1), 0)
    keep = (row < size_ref[0]).astype(jnp.float32)
    high_ref[...], low_ref[...] = split(left_ref[...] * mask_ref[...] * keep)


def prepare(left, colmask, size):
    col, al, depth = left.shape
    rows, block = col * al, 128
    return pl.pallas_call(
        prepare_kernel,
        grid_spec=pltpu.PrefetchScalarGridSpec(
            num_scalar_prefetch=1,
            grid=(rows // block,),
            in_specs=[
                pl.BlockSpec((block, depth), lambda n, *_: (n, 0)),
                pl.BlockSpec((1, depth), lambda n, *_: (0, 0)),
            ],
            out_specs=[pl.BlockSpec((block, depth), lambda n, *_: (n, 0))] * 2,
        ),
        out_shape=[jax.ShapeDtypeStruct((rows, depth), jnp.bfloat16)] * 2,
        compiler_params=pltpu.CompilerParams(vmem_limit_bytes=56 * MIB),
        cost_estimate=pl.CostEstimate(flops=4 * rows * depth, bytes_accessed=8 * rows * depth, transcendentals=0),
    )(size, left.reshape(rows, depth), colmask)


def multiply_kernel(*refs, panels, lefts):
    order_ref, left_refs = refs[0], refs[1:1 + 2 * lefts]
    panel_refs, out_ref = refs[1 + 2 * lefts:-1], refs[-1]
    del order_ref
    high, low = split(jnp.concatenate([ref[...].reshape(ref.shape[-2:]) for ref in panel_refs], axis=0))
    dot = functools.partial(jnp.dot, preferred_element_type=jnp.float32)
    for i in range(lefts):
        left_high, left_low = left_refs[2 * i], left_refs[2 * i + 1]
        total = dot(left_high[...], high) + (dot(left_high[...], low) + dot(left_low[...], high))
        out_ref[:, i] = total.reshape(out_ref.shape[0], *out_ref.shape[2:])


def multiply(order, lefts, panels, virtuals):
    rows, depth = lefts[0].shape
    width = panels[0].shape[-1]
    count = len(lefts) // 2
    if len(panels) == 1:
        blocks = panels[0].shape[0]
        panels = panels * blocks
        specs = [
            pl.BlockSpec((1, depth // blocks, TILE), lambda n, o, i=i: (o[i], 0, n)) for i in range(blocks)
        ]
    else:
        specs = [pl.BlockSpec((panel.shape[0], TILE), lambda n, o: (0, n)) for panel in panels]
    shape = (rows // virtuals, count, virtuals)
    return pl.pallas_call(
        functools.partial(multiply_kernel, panels=len(panels), lefts=count),
        grid_spec=pltpu.PrefetchScalarGridSpec(
            num_scalar_prefetch=1,
            grid=(width // TILE,),
            in_specs=[pl.BlockSpec((rows, depth), lambda n, o: (0, 0))] * (2 * count) + specs,
            out_specs=pl.BlockSpec((*shape, TILE), lambda n, o: (0, 0, 0, n)),
        ),
        out_shape=jax.ShapeDtypeStruct((*shape, width), jnp.float32),
        compiler_params=pltpu.CompilerParams(vmem_limit_bytes=56 * MIB),
        cost_estimate=pl.CostEstimate(
            flops=6 * count * rows * depth * width,
            bytes_accessed=4 * (count * rows * depth + depth * width + count * rows * width),
            transcendentals=0,
        ),
    )(order, *lefts, *panels)


def body(amplitudes, integrals, occ_irrep, vir_irrep):
    rows, col = lax.axis_size("row"), lax.axis_size("col")
    wl, kt, al, ct = amplitudes.shape
    kl, cl, nt = integrals.shape
    part, chips = kl // 2, rows // 2
    cross = [(r, r ^ 1) for r in range(rows)]
    up = [(r, (r + 2) % rows) for r in range(rows)]
    down = [(r, (r - 2) % rows) for r in range(rows)]
    here = lax.axis_index("row")
    chip, core = here // 2, here % 2
    order = jnp.stack(
        [(chip + s) % chips * 2 + c for c in (core, 1 - core) for s in (0, chips - 1, 1, 2)]
    ).astype(jnp.int32)

    def to_rows(value):
        return lax.all_to_all(value, "col", split_axis=0, concat_axis=0, tiled=True)

    def ring(value):
        return [lax.ppermute(value, "row", up), lax.ppermute(value, "row", down)]

    def ring_on(near):
        return [lax.ppermute(near[0][:part], "row", up), lax.ppermute(near[1][part:], "row", down)]

    def other_core(values):
        return [lax.ppermute(value, "row", cross) for value in values]

    def flat(*panels):
        return [panel.reshape(-1, panel.shape[-1]) for panel in panels]

    packed = [pack(amplitudes, order, kl, cl, w) for w in range(wl)]
    late, early = integrals[:, :, :WIDTHS[1]], integrals[:, :, WIDTHS[1]:]
    near0 = ring(early)
    near0, packed[1] = lax.optimization_barrier((near0, packed[1]))
    far0 = ring_on(near0)
    over0 = other_core([early, *near0])
    colmask, row_sizes = masks(kt, wl, cl, occ_irrep, vir_irrep)
    colmask = colmask.reshape(rows, kl * cl)
    colmask = jnp.concatenate([lax.dynamic_slice_in_dim(colmask, order[i], 1) for i in range(rows)], axis=1)
    left0 = to_rows(packed[0])
    packed[1], left0 = lax.optimization_barrier((packed[1], left0))
    left1 = to_rows(packed[1])
    halves = prepare(left0, colmask, row_sizes[0:1])
    (far0, over0) = lax.optimization_barrier((far0, over0, halves))[:2]
    (late, far0, over0) = lax.optimization_barrier((late, far0, over0))
    near1 = ring(late)
    over0 += other_core(far0)
    panels = flat(early, *near0, *far0, *over0)
    piece0 = multiply(order, halves, panels, al)
    moved0 = to_rows(lax.optimization_barrier((piece0, left1))[0])
    halves = halves + prepare(left1, colmask, row_sizes[1:2])
    piece1 = multiply(order, halves[2:], panels, al)
    near1 = lax.optimization_barrier((near1, piece1))[0]
    far1 = ring_on(near1)
    over1 = other_core([late, *near1])
    far1 = lax.optimization_barrier((far1, piece1))[0]
    over1 += other_core(far1)
    last = multiply(order, halves, flat(late, *near1, *far1, *over1), al)
    moved1 = to_rows(lax.optimization_barrier((piece1, moved0))[0])
    last = lax.optimization_barrier((last, moved1))[0]
    sums = [jnp.sum(moved, axis=0) for moved in (moved0, moved1)]
    last = jnp.sum(to_rows(last), axis=0)
    return jnp.concatenate([last, jnp.concatenate(sums, axis=0)], axis=2)


def solution(mesh):
    return jax.shard_map(
        body,
        mesh=mesh,
        in_specs=(P("row", None, "col", None), P("row", "col", None), P(), P()),
        out_specs=P("row", "col", None),
        check_vma=False,
    )
```

```python
import functools

import jax
import jax.numpy as jnp
from jax import lax
from jax.experimental import pallas as pl
from jax.experimental.pallas import tpu as pltpu
from jax.sharding import PartitionSpec as P

WIDTHS = (1536, 1024)
TILE = 256
LANES = 128
MIB = 1024 * 1024


def irrep_counts(vir_irrep):
    labels = jnp.arange(8, dtype=jnp.int32)
    return jnp.sum((vir_irrep[:, None] == labels[None, :]).astype(jnp.int32), axis=0)


def block_sizes(orbital_irreps, counts):
    labels = jnp.arange(8, dtype=jnp.int32)
    return jnp.sum(
        jnp.where(orbital_irreps[:, None] == labels[None, :], counts[None, :], 0), axis=1
    )


def masks(slot_total, local_orbitals, local_columns, occ_irrep, vir_irrep):
    occupied = occ_irrep.shape[0]
    window_total = local_orbitals * lax.axis_size("row")
    counts = irrep_counts(vir_irrep)
    sizes = jnp.pad(block_sizes(occ_irrep, counts), (0, slot_total - occupied))
    local = lax.axis_index("col") * local_columns + jnp.arange(local_columns, dtype=jnp.int32)
    colmask = (local[None, :] < sizes[:, None]).astype(jnp.float32).reshape(1, slot_total * local_columns)
    window = lax.axis_index("row") * local_orbitals + jnp.arange(local_orbitals, dtype=jnp.int32)
    orbital = window * occupied // window_total
    matches = jnp.arange(occupied, dtype=jnp.int32)[None, :] == orbital[:, None]
    row_sizes = block_sizes(jnp.sum(jnp.where(matches, occ_irrep[None, :], 0), axis=1), counts)
    return colmask, row_sizes


def pack_kernel(order_ref, first_ref, second_ref, out_ref, *, width):
    slots, rows, columns = first_ref.shape[1:]
    per = LANES // width
    place = lax.broadcasted_iota(jnp.int32, (rows, LANES), 1) // width
    for group in range(2 * slots // per):
        for half in range(columns // LANES):
            at = slice(half * LANES, (half + 1) * LANES)
            tiles = []
            for k in range(per):
                slot = group * per + k
                ref = first_ref if slot < slots else second_ref
                tile = ref[0, slot % slots, :, at]
                tiles.append(pltpu.roll(tile, k * width, 1) if k else tile)
            span = 1
            while span < per:
                taken = place & span != 0
                tiles = [jnp.where(taken, tiles[(h + span) % per], tiles[h]) for h in range(per)]
                span *= 2
            for g in range(per):
                tile = tiles[-g % per]
                tile = pltpu.roll(tile, LANES - g * width, 1) if g else tile
                out_ref[half * per + g, :, group * LANES:(group + 1) * LANES] = tile


def pack(amplitudes, order, slots, width, orbital):
    wl, kt, al, ct = amplitudes.shape
    return pl.pallas_call(
        functools.partial(pack_kernel, width=width),
        grid_spec=pltpu.PrefetchScalarGridSpec(
            num_scalar_prefetch=1,
            grid=(kt // slots // 2,),
            in_specs=[
                pl.BlockSpec((1, slots, al, ct), lambda p, o: (orbital, o[2 * p], 0, 0)),
                pl.BlockSpec((1, slots, al, ct), lambda p, o: (orbital, o[2 * p + 1], 0, 0)),
            ],
            out_specs=pl.BlockSpec((ct // width, al, 2 * slots * width), lambda p, o: (0, 0, p)),
        ),
        out_shape=jax.ShapeDtypeStruct((ct // width, al, kt * width), jnp.float32),
        compiler_params=pltpu.CompilerParams(vmem_limit_bytes=56 * MIB),
        cost_estimate=pl.CostEstimate(
            flops=kt * al * ct, bytes_accessed=8 * kt * al * ct, transcendentals=0
        ),
    )(order, amplitudes, amplitudes)


def split(value):
    high = value.astype(jnp.bfloat16)
    return high, (value - high.astype(jnp.float32)).astype(jnp.bfloat16)


def prepare_kernel(size_ref, left_ref, mask_ref, high_ref, low_ref):
    block = left_ref.shape[0]
    row = pl.program_id(0) * block + lax.broadcasted_iota(jnp.int32, (block, 1), 0)
    keep = (row < size_ref[0]).astype(jnp.float32)
    high_ref[...], low_ref[...] = split(left_ref[...] * mask_ref[...] * keep)


def prepare(left, colmask, size):
    col, al, depth = left.shape
    rows, block = col * al, 128
    return pl.pallas_call(
        prepare_kernel,
        grid_spec=pltpu.PrefetchScalarGridSpec(
            num_scalar_prefetch=1,
            grid=(rows // block,),
            in_specs=[
                pl.BlockSpec((block, depth), lambda n, *_: (n, 0)),
                pl.BlockSpec((1, depth), lambda n, *_: (0, 0)),
            ],
            out_specs=[pl.BlockSpec((block, depth), lambda n, *_: (n, 0))] * 2,
        ),
        out_shape=[jax.ShapeDtypeStruct((rows, depth), jnp.bfloat16)] * 2,
        compiler_params=pltpu.CompilerParams(vmem_limit_bytes=56 * MIB),
        cost_estimate=pl.CostEstimate(flops=4 * rows * depth, bytes_accessed=8 * rows * depth, transcendentals=0),
    )(size, left.reshape(rows, depth), colmask)


def multiply_kernel(*refs, panels, lefts):
    order_ref, left_refs = refs[0], refs[1:1 + 2 * lefts]
    panel_refs, out_ref = refs[1 + 2 * lefts:-1], refs[-1]
    del order_ref
    high, low = split(jnp.concatenate([ref[...].reshape(ref.shape[-2:]) for ref in panel_refs], axis=0))
    dot = functools.partial(jnp.dot, preferred_element_type=jnp.float32)
    for i in range(lefts):
        left_high, left_low = left_refs[2 * i], left_refs[2 * i + 1]
        total = dot(left_high[...], high) + (dot(left_high[...], low) + dot(left_low[...], high))
        out_ref[:, i] = total.reshape(out_ref.shape[0], *out_ref.shape[2:])


def multiply(order, lefts, panels, virtuals):
    rows, depth = lefts[0].shape
    width = panels[0].shape[-1]
    count = len(lefts) // 2
    if len(panels) == 1:
        blocks = panels[0].shape[0]
        panels = panels * blocks
        specs = [
            pl.BlockSpec((1, depth // blocks, TILE), lambda n, o, i=i: (o[i], 0, n)) for i in range(blocks)
        ]
    else:
        specs = [pl.BlockSpec((panel.shape[0], TILE), lambda n, o: (0, n)) for panel in panels]
    shape = (rows // virtuals, count, virtuals)
    return pl.pallas_call(
        functools.partial(multiply_kernel, panels=len(panels), lefts=count),
        grid_spec=pltpu.PrefetchScalarGridSpec(
            num_scalar_prefetch=1,
            grid=(width // TILE,),
            in_specs=[pl.BlockSpec((rows, depth), lambda n, o: (0, 0))] * (2 * count) + specs,
            out_specs=pl.BlockSpec((*shape, TILE), lambda n, o: (0, 0, 0, n)),
        ),
        out_shape=jax.ShapeDtypeStruct((*shape, width), jnp.float32),
        compiler_params=pltpu.CompilerParams(vmem_limit_bytes=56 * MIB),
        cost_estimate=pl.CostEstimate(
            flops=6 * count * rows * depth * width,
            bytes_accessed=4 * (count * rows * depth + depth * width + count * rows * width),
            transcendentals=0,
        ),
    )(order, *lefts, *panels)


def halve_kernel(above_ref, below_ref, first_ref, second_ref):
    first_ref[...] = above_ref[...]
    second_ref[...] = below_ref[...]


def halve(above, below):
    slots, rows, width = above.shape
    half, block = slots // 2, slots // 4
    shape = jax.ShapeDtypeStruct((half, rows, width), above.dtype)
    return pl.pallas_call(
        halve_kernel,
        grid=(half // block,),
        in_specs=[
            pl.BlockSpec((block, rows, width), lambda n: (n, 0, 0)),
            pl.BlockSpec((block, rows, width), lambda n: (n + half // block, 0, 0)),
        ],
        out_specs=[pl.BlockSpec((block, rows, width), lambda n: (n, 0, 0))] * 2,
        out_shape=[shape] * 2,
        compiler_params=pltpu.CompilerParams(vmem_limit_bytes=56 * MIB),
        cost_estimate=pl.CostEstimate(flops=0, bytes_accessed=16 * half * rows * width, transcendentals=0),
    )(above, below)


def body(amplitudes, integrals, occ_irrep, vir_irrep):
    rows, col = lax.axis_size("row"), lax.axis_size("col")
    wl, kt, al, ct = amplitudes.shape
    kl, cl, nt = integrals.shape
    chips = rows // 2
    cross = [(r, r ^ 1) for r in range(rows)]
    up = [(r, (r + 2) % rows) for r in range(rows)]
    down = [(r, (r - 2) % rows) for r in range(rows)]
    here = lax.axis_index("row")
    chip, core = here // 2, here % 2
    order = jnp.stack(
        [(chip + s) % chips * 2 + c for c in (core, 1 - core) for s in (0, chips - 1, 1, 2)]
    ).astype(jnp.int32)

    def to_rows(value):
        return lax.all_to_all(value, "col", split_axis=0, concat_axis=0, tiled=True)

    def ring(value):
        return [lax.ppermute(value, "row", up), lax.ppermute(value, "row", down)]

    def ring_on(near):
        first, second = halve(*near)
        return [lax.ppermute(first, "row", up), lax.ppermute(second, "row", down)]

    def other_core(values):
        return [lax.ppermute(value, "row", cross) for value in values]

    def flat(*panels):
        return [panel.reshape(-1, panel.shape[-1]) for panel in panels]

    packed = [pack(amplitudes, order, kl, cl, w) for w in range(wl)]
    late, early = integrals[:, :, :WIDTHS[1]], integrals[:, :, WIDTHS[1]:]
    near0 = ring(early)
    near0, packed[1] = lax.optimization_barrier((near0, packed[1]))
    far0 = ring_on(near0)
    over0 = other_core([early, *near0])
    colmask, row_sizes = masks(kt, wl, cl, occ_irrep, vir_irrep)
    colmask = colmask.reshape(rows, kl * cl)
    colmask = jnp.concatenate([lax.dynamic_slice_in_dim(colmask, order[i], 1) for i in range(rows)], axis=1)
    left0 = to_rows(packed[0])
    left1 = to_rows(lax.optimization_barrier((packed[1], left0))[0])
    halves = prepare(left0, colmask, row_sizes[0:1])
    (far0, over0) = lax.optimization_barrier((far0, over0, halves))[:2]
    (late, far0, over0) = lax.optimization_barrier((late, far0, over0))
    near1 = ring(late)
    over0 += other_core(far0)
    panels = flat(early, *near0, *far0, *over0)
    piece0 = multiply(order, halves, panels, al)
    moved0 = to_rows(lax.optimization_barrier((piece0, left1))[0])
    halves = halves + prepare(left1, colmask, row_sizes[1:2])
    near1 = lax.optimization_barrier((near1, piece0, halves[2:]))[0]
    far1 = ring_on(near1)
    piece1 = multiply(order, halves[2:], panels, al)
    over1 = other_core([late, *near1])
    far1 = lax.optimization_barrier((far1, piece1))[0]
    over1 += other_core(far1)
    last = multiply(order, halves, flat(late, *near1, *far1, *over1), al)
    moved1 = to_rows(lax.optimization_barrier((piece1, moved0))[0])
    last = lax.optimization_barrier((last, moved1))[0]
    sums = [jnp.sum(moved, axis=0) for moved in (moved0, moved1)]
    last = jnp.sum(to_rows(last), axis=0)
    return jnp.concatenate([last, jnp.concatenate(sums, axis=0)], axis=2)


def solution(mesh):
    return jax.shard_map(
        body,
        mesh=mesh,
        in_specs=(P("row", None, "col", None), P("row", "col", None), P(), P()),
        out_specs=P("row", "col", None),
        check_vma=False,
    )
```

```python
import functools

import jax
import jax.numpy as jnp
from jax import lax
from jax.experimental import pallas as pl
from jax.experimental.pallas import tpu as pltpu
from jax.sharding import PartitionSpec as P

WIDTHS = (1536, 1024)
TILE = 256
LANES = 128
MIB = 1024 * 1024


def irrep_counts(vir_irrep):
    labels = jnp.arange(8, dtype=jnp.int32)
    return jnp.sum((vir_irrep[:, None] == labels[None, :]).astype(jnp.int32), axis=0)


def block_sizes(orbital_irreps, counts):
    labels = jnp.arange(8, dtype=jnp.int32)
    return jnp.sum(
        jnp.where(orbital_irreps[:, None] == labels[None, :], counts[None, :], 0), axis=1
    )


def masks(slot_total, local_orbitals, local_columns, occ_irrep, vir_irrep):
    occupied = occ_irrep.shape[0]
    window_total = local_orbitals * lax.axis_size("row")
    counts = irrep_counts(vir_irrep)
    sizes = jnp.pad(block_sizes(occ_irrep, counts), (0, slot_total - occupied))
    local = lax.axis_index("col") * local_columns + jnp.arange(local_columns, dtype=jnp.int32)
    colmask = (local[None, :] < sizes[:, None]).astype(jnp.float32).reshape(1, slot_total * local_columns)
    window = lax.axis_index("row") * local_orbitals + jnp.arange(local_orbitals, dtype=jnp.int32)
    orbital = window * occupied // window_total
    matches = jnp.arange(occupied, dtype=jnp.int32)[None, :] == orbital[:, None]
    row_sizes = block_sizes(jnp.sum(jnp.where(matches, occ_irrep[None, :], 0), axis=1), counts)
    return colmask, row_sizes


def pack_kernel(order_ref, first_ref, second_ref, out_ref, *, width):
    slots, rows, columns = first_ref.shape[1:]
    per = LANES // width
    place = lax.broadcasted_iota(jnp.int32, (rows, LANES), 1) // width
    for group in range(2 * slots // per):
        for half in range(columns // LANES):
            at = slice(half * LANES, (half + 1) * LANES)
            tiles = []
            for k in range(per):
                slot = group * per + k
                ref = first_ref if slot < slots else second_ref
                tile = ref[0, slot % slots, :, at]
                tiles.append(pltpu.roll(tile, k * width, 1) if k else tile)
            span = 1
            while span < per:
                taken = place & span != 0
                tiles = [jnp.where(taken, tiles[(h + span) % per], tiles[h]) for h in range(per)]
                span *= 2
            for g in range(per):
                tile = tiles[-g % per]
                tile = pltpu.roll(tile, LANES - g * width, 1) if g else tile
                out_ref[half * per + g, :, group * LANES:(group + 1) * LANES] = tile


def pack(amplitudes, order, slots, width, orbital):
    wl, kt, al, ct = amplitudes.shape
    return pl.pallas_call(
        functools.partial(pack_kernel, width=width),
        grid_spec=pltpu.PrefetchScalarGridSpec(
            num_scalar_prefetch=1,
            grid=(kt // slots // 2,),
            in_specs=[
                pl.BlockSpec((1, slots, al, ct), lambda p, o: (orbital, o[2 * p], 0, 0)),
                pl.BlockSpec((1, slots, al, ct), lambda p, o: (orbital, o[2 * p + 1], 0, 0)),
            ],
            out_specs=pl.BlockSpec((ct // width, al, 2 * slots * width), lambda p, o: (0, 0, p)),
        ),
        out_shape=jax.ShapeDtypeStruct((ct // width, al, kt * width), jnp.float32),
        compiler_params=pltpu.CompilerParams(vmem_limit_bytes=56 * MIB),
        cost_estimate=pl.CostEstimate(
            flops=kt * al * ct, bytes_accessed=8 * kt * al * ct, transcendentals=0
        ),
    )(order, amplitudes, amplitudes)


def split(value):
    high = value.astype(jnp.bfloat16)
    return high, (value - high.astype(jnp.float32)).astype(jnp.bfloat16)


def prepare_kernel(size_ref, left_ref, mask_ref, high_ref, low_ref):
    block = left_ref.shape[0]
    row = pl.program_id(0) * block + lax.broadcasted_iota(jnp.int32, (block, 1), 0)
    keep = (row < size_ref[0]).astype(jnp.float32)
    high_ref[...], low_ref[...] = split(left_ref[...] * mask_ref[...] * keep)


def prepare(left, colmask, size):
    col, al, depth = left.shape
    rows, block = col * al, 128
    return pl.pallas_call(
        prepare_kernel,
        grid_spec=pltpu.PrefetchScalarGridSpec(
            num_scalar_prefetch=1,
            grid=(rows // block,),
            in_specs=[
                pl.BlockSpec((block, depth), lambda n, *_: (n, 0)),
                pl.BlockSpec((1, depth), lambda n, *_: (0, 0)),
            ],
            out_specs=[pl.BlockSpec((block, depth), lambda n, *_: (n, 0))] * 2,
        ),
        out_shape=[jax.ShapeDtypeStruct((rows, depth), jnp.bfloat16)] * 2,
        compiler_params=pltpu.CompilerParams(vmem_limit_bytes=56 * MIB),
        cost_estimate=pl.CostEstimate(flops=4 * rows * depth, bytes_accessed=8 * rows * depth, transcendentals=0),
    )(size, left.reshape(rows, depth), colmask)


def multiply_kernel(*refs, panels, lefts):
    order_ref, left_refs = refs[0], refs[1:1 + 2 * lefts]
    panel_refs, out_ref = refs[1 + 2 * lefts:-1], refs[-1]
    del order_ref
    high, low = split(jnp.concatenate([ref[...].reshape(ref.shape[-2:]) for ref in panel_refs], axis=0))
    dot = functools.partial(jnp.dot, preferred_element_type=jnp.float32)
    for i in range(lefts):
        left_high, left_low = left_refs[2 * i], left_refs[2 * i + 1]
        total = dot(left_high[...], high) + (dot(left_high[...], low) + dot(left_low[...], high))
        out_ref[:, i] = total.reshape(out_ref.shape[0], *out_ref.shape[2:])


def multiply(order, lefts, panels, virtuals):
    rows, depth = lefts[0].shape
    width = panels[0].shape[-1]
    count = len(lefts) // 2
    if len(panels) == 1:
        blocks = panels[0].shape[0]
        panels = panels * blocks
        specs = [
            pl.BlockSpec((1, depth // blocks, TILE), lambda n, o, i=i: (o[i], 0, n)) for i in range(blocks)
        ]
    else:
        specs = [pl.BlockSpec((panel.shape[0], TILE), lambda n, o: (0, n)) for panel in panels]
    shape = (rows // virtuals, count, virtuals)
    return pl.pallas_call(
        functools.partial(multiply_kernel, panels=len(panels), lefts=count),
        grid_spec=pltpu.PrefetchScalarGridSpec(
            num_scalar_prefetch=1,
            grid=(width // TILE,),
            in_specs=[pl.BlockSpec((rows, depth), lambda n, o: (0, 0))] * (2 * count) + specs,
            out_specs=pl.BlockSpec((*shape, TILE), lambda n, o: (0, 0, 0, n)),
        ),
        out_shape=jax.ShapeDtypeStruct((*shape, width), jnp.float32),
        compiler_params=pltpu.CompilerParams(vmem_limit_bytes=56 * MIB),
        cost_estimate=pl.CostEstimate(
            flops=6 * count * rows * depth * width,
            bytes_accessed=4 * (count * rows * depth + depth * width + count * rows * width),
            transcendentals=0,
        ),
    )(order, *lefts, *panels)


def multiply_raw_kernel(size_ref, left_ref, mask_ref, *refs):
    panel_refs, (out_ref, left_high, left_low) = refs[:-3], refs[-3:]
    block = 64

    @pl.when(pl.program_id(0) == 0)
    def _():
        for start in range(0, left_ref.shape[0], block):
            at = slice(start, start + block)
            row = start + lax.broadcasted_iota(jnp.int32, (block, 1), 0)
            keep = (row < size_ref[0]).astype(jnp.float32)
            left_high[at], left_low[at] = split(left_ref[at] * mask_ref[...] * keep)

    high, low = split(jnp.concatenate([ref[...] for ref in panel_refs], axis=0))
    dot = functools.partial(jnp.dot, preferred_element_type=jnp.float32)
    total = dot(left_high[...], high) + (dot(left_high[...], low) + dot(left_low[...], high))
    out_ref[:, 0] = total.reshape(out_ref.shape[0], *out_ref.shape[2:])


def multiply_raw(left, colmask, size, panels):
    col, al, depth = left.shape
    rows, width = col * al, panels[0].shape[1]
    return pl.pallas_call(
        multiply_raw_kernel,
        grid_spec=pltpu.PrefetchScalarGridSpec(
            num_scalar_prefetch=1,
            grid=(width // TILE,),
            in_specs=[
                pl.BlockSpec((rows, depth), lambda n, s: (0, 0)),
                pl.BlockSpec((1, depth), lambda n, s: (0, 0)),
            ]
            + [pl.BlockSpec((panel.shape[0], TILE), lambda n, s: (0, n)) for panel in panels],
            out_specs=pl.BlockSpec((col, 1, al, TILE), lambda n, s: (0, 0, 0, n)),
            scratch_shapes=[pltpu.VMEM((rows, depth), jnp.bfloat16)] * 2,
        ),
        out_shape=jax.ShapeDtypeStruct((col, 1, al, width), jnp.float32),
        compiler_params=pltpu.CompilerParams(vmem_limit_bytes=56 * MIB),
        cost_estimate=pl.CostEstimate(
            flops=6 * rows * depth * width,
            bytes_accessed=4 * (rows * depth + depth * width + rows * width),
            transcendentals=0,
        ),
    )(size, left.reshape(rows, depth), colmask, *panels)


def halve_kernel(above_ref, below_ref, first_ref, second_ref):
    first_ref[...] = above_ref[...]
    second_ref[...] = below_ref[...]


def halve(above, below):
    slots, rows, width = above.shape
    half, block = slots // 2, slots // 4
    shape = jax.ShapeDtypeStruct((half, rows, width), above.dtype)
    return pl.pallas_call(
        halve_kernel,
        grid=(half // block,),
        in_specs=[
            pl.BlockSpec((block, rows, width), lambda n: (n, 0, 0)),
            pl.BlockSpec((block, rows, width), lambda n: (n + half // block, 0, 0)),
        ],
        out_specs=[pl.BlockSpec((block, rows, width), lambda n: (n, 0, 0))] * 2,
        out_shape=[shape] * 2,
        compiler_params=pltpu.CompilerParams(vmem_limit_bytes=56 * MIB),
        cost_estimate=pl.CostEstimate(flops=0, bytes_accessed=16 * half * rows * width, transcendentals=0),
    )(above, below)


def body(amplitudes, integrals, occ_irrep, vir_irrep):
    rows, col = lax.axis_size("row"), lax.axis_size("col")
    wl, kt, al, ct = amplitudes.shape
    kl, cl, nt = integrals.shape
    chips = rows // 2
    cross = [(r, r ^ 1) for r in range(rows)]
    up = [(r, (r + 2) % rows) for r in range(rows)]
    down = [(r, (r - 2) % rows) for r in range(rows)]
    here = lax.axis_index("row")
    chip, core = here // 2, here % 2
    order = jnp.stack(
        [(chip + s) % chips * 2 + c for c in (core, 1 - core) for s in (0, chips - 1, 1, 2)]
    ).astype(jnp.int32)

    def to_rows(value):
        return lax.all_to_all(value, "col", split_axis=0, concat_axis=0, tiled=True)

    def ring(value):
        return [lax.ppermute(value, "row", up), lax.ppermute(value, "row", down)]

    def ring_on(near):
        first, second = halve(*near)
        return [lax.ppermute(first, "row", up), lax.ppermute(second, "row", down)]

    def other_core(values):
        return [lax.ppermute(value, "row", cross) for value in values]

    def flat(*panels):
        return [panel.reshape(-1, panel.shape[-1]) for panel in panels]

    packed = [pack(amplitudes, order, kl, cl, w) for w in range(wl)]
    late, early = integrals[:, :, :WIDTHS[1]], integrals[:, :, WIDTHS[1]:]
    near0 = ring(early)
    near0, packed[1] = lax.optimization_barrier((near0, packed[1]))
    far0 = ring_on(near0)
    over0 = other_core([early, *near0])
    colmask, row_sizes = masks(kt, wl, cl, occ_irrep, vir_irrep)
    colmask = colmask.reshape(rows, kl * cl)
    colmask = jnp.concatenate([lax.dynamic_slice_in_dim(colmask, order[i], 1) for i in range(rows)], axis=1)
    left0 = to_rows(packed[0])
    left1 = to_rows(lax.optimization_barrier((packed[1], left0))[0])
    halves = prepare(left0, colmask, row_sizes[0:1])
    (far0, over0) = lax.optimization_barrier((far0, over0, halves))[:2]
    (late, far0, over0) = lax.optimization_barrier((late, far0, over0))
    near1 = ring(late)
    over0 += other_core(far0)
    panels = flat(early, *near0, *far0, *over0)
    piece0 = multiply(order, halves, panels, al)
    moved0 = to_rows(lax.optimization_barrier((piece0, left1))[0])
    piece1 = multiply_raw(left1, colmask, row_sizes[1:2], panels)
    halves = halves + prepare(lax.optimization_barrier((left1, piece1))[0], colmask, row_sizes[1:2])
    near1 = lax.optimization_barrier((near1, piece1))[0]
    far1 = ring_on(near1)
    over1 = other_core([late, *near1])
    far1 = lax.optimization_barrier((far1, piece1))[0]
    over1 += other_core(far1)
    last = multiply(order, halves, flat(late, *near1, *far1, *over1), al)
    moved1 = to_rows(lax.optimization_barrier((piece1, moved0))[0])
    last = lax.optimization_barrier((last, moved1))[0]
    sums = [jnp.sum(moved, axis=0) for moved in (moved0, moved1)]
    last = jnp.sum(to_rows(last), axis=0)
    return jnp.concatenate([last, jnp.concatenate(sums, axis=0)], axis=2)


def solution(mesh):
    return jax.shard_map(
        body,
        mesh=mesh,
        in_specs=(P("row", None, "col", None), P("row", "col", None), P(), P()),
        out_specs=P("row", "col", None),
        check_vma=False,
    )
```
